256 devices in a mesh: wave: 64 (over x, z, core), lev: 4 (over y).
Axes of the slice: x: 4, y: 4, z: 8, core: 2. Of those that a mesh axis runs over, the one named last changes fastest.
Arguments:
- spectra: bfloat16 [640, 2, 3, 128, 640], P('wave', None, None, 'lev'), may hold values from -0.15625 to 0.15625
- legendre_table: bfloat16 [640, 640, 512], P('wave'), may hold values from -0.25 to 0.25
- m_order: int32 [640], replicated, may hold values from 0 to 639, as said below
- row_points: int32 [512], replicated, may hold values from 20 to 2576, as said below
Outputs:
- grid: bfloat16 [512, 3, 128, 2688], P(('wave', 'lev'))
The draws below stay inside these ranges and needn't reach their ends.
Inputs may be any that keep to these rules, and one draw needn't show every extreme that they name: `m_order`: A permutation of 0 to 639. Entries 2 i and 2 i + 1 are a and 639 - a with a < 320. `row_points`: each is 20 + 4 min(i, 1279 - i) for the row's latitude index i from the pole; some row lies at the equator.
All inputs are finite; a program needn't handle non-finite values.
Results may differ from the reference program's by a relative error of at most 0.0055.
Values may be sent and summed in bfloat16 or wider, within the bound.
A program may use at most 128 MiB of HBM per device.

```python
import math
import jax
import jax.numpy as jnp
from jax import lax

TRUNC = 639
ROWPAD = 2688
FLDS = 3
M = 640
LEV = 128
NLAT = 512


def draw_m_order(key, part):
    key = jax.random.fold_in(key, 11)
    low_half = jax.random.permutation(key, M // 2).astype(jnp.int32)
    return jnp.stack([low_half, M - 1 - low_half], axis=1).reshape(M).astype(jnp.int32)


def draw_row_points(key, part):
    key = jax.random.fold_in(key, 23)
    row_key, slot_key = jax.random.split(key)
    lat_rows = jax.random.randint(row_key, (NLAT,), 0, 2 * M)
    equator_slot = jax.random.randint(slot_key, (), 0, NLAT)
    lat_rows = jnp.where(jnp.arange(NLAT) == equator_slot, TRUNC, lat_rows)
    return (20 + 4 * jnp.minimum(lat_rows, 2 * M - 1 - lat_rows)).astype(jnp.int32)


def level_of(own_key, dims, cuts, smallest, high):
    gain = 1.0
    for position, blocks in cuts:
        heights = jax.random.uniform(jax.random.fold_in(jax.random.fold_in(own_key, 6), position), (blocks,), jnp.float32, smallest / len(cuts), high / len(cuts))
        gain = gain * jnp.repeat(jnp.exp(heights), dims[position] // blocks).reshape((-1,) + (1,) * (len(dims) - 1 - position))
    return gain


def normal_values(rng, dims, scale, bound, shards=(), kind=jnp.bfloat16):
    drawn = jax.random.normal(rng, dims, jnp.float32) * scale
    if len(shards) > 0:
        drawn = level_of(rng, dims, shards, -0.22, 0.18) * drawn
    return jnp.clip(drawn, min=-bound, max=bound).astype(kind)


def setup_inputs(seed: int = 0) -> dict:
    seeds = jax.random.split(jax.random.key(seed), 5)
    return {
        "spectra": normal_values(seeds[0], (M, 2, FLDS, LEV, M), (1.0 / (2 * M) ** 0.5), 0.15625, ((0, 64), (3, 4))),
        "legendre_table": normal_values(seeds[1], (M, M, NLAT), M ** -0.5, 0.25, ((0, 64),)),
        "m_order": draw_m_order(jax.random.fold_in(seeds[4], 71), 0),
        "row_points": draw_row_points(jax.random.fold_in(seeds[4], 71), 0),
    }


def synthesis_basis(wavenumbers, points, width):
    column = wavenumbers[:, None]
    longitude = lax.iota(jnp.int32, width)[None, :]
    residue = (column * longitude) % points
    folded = jnp.minimum(residue, points - residue)
    angle = folded.astype(jnp.float32) * (2.0 * math.pi) / points.astype(jnp.float32)
    orient = jnp.where(2 * residue <= points, 1.0, -1.0).astype(jnp.float32)
    active = (2 * column < points) & (longitude < points)
    factor = jnp.where(active, jnp.where(column == 0, 1.0, 2.0), 0.0).astype(jnp.float32)
    cosine = (factor * jnp.cos(angle)).astype(jnp.bfloat16)
    sine = (-(factor * orient) * jnp.sin(angle)).astype(jnp.bfloat16)
    return cosine, sine


def trim_spectra(spectra, wavenumbers):
    degree = lax.iota(jnp.int32, spectra.shape[-1])
    keep = degree[None, :] < (spectra.shape[-1] - wavenumbers)[:, None]
    return jnp.where(keep[:, None, None, None, :], spectra, jnp.zeros((), spectra.dtype))


def reference(spectra, legendre_table, m_order, row_points):
    trimmed = trim_spectra(spectra, m_order)

    def one_wave(pair):
        coeff, table = pair
        return jnp.einsum('cflk,kj->jcfl', coeff.astype(jnp.float32), table.astype(jnp.float32),
                          precision=lax.Precision.HIGHEST).astype(jnp.bfloat16)

    waves = lax.map(one_wave, (trimmed, legendre_table))
    columns = jnp.transpose(waves, (1, 2, 0, 3, 4)).reshape(NLAT, 2 * M, FLDS * LEV)

    def one_row(pair):
        coeff, points = pair
        cosine, sine = synthesis_basis(m_order, points, ROWPAD)
        basis = jnp.concatenate([cosine, sine], axis=0)
        field = jnp.dot(coeff.T, basis, preferred_element_type=jnp.float32)
        return field.astype(jnp.bfloat16).reshape(FLDS, LEV, ROWPAD)

    return lax.map(one_row, (columns, row_points))
```

```python
import functools
import math

import jax
import jax.numpy as jnp
import numpy as np
from jax import lax
from jax.experimental import pallas as pl
from jax.experimental.pallas import tpu as pltpu
from jax.sharding import PartitionSpec as P

MESH = pl.DeviceIdType.MESH
NX, NY, NZ, NC = 4, 4, 8, 2
NPEER = NX * NY * NC
WAVES = 10
PAIRS = WAVES // 2
FL = 96
PAIR_LANES = 4 * FL
LANES = PAIRS * PAIR_LANES
DEG = 640
NLAT = 512
ROWPAD = 2688
TILES = ROWPAD // 128
KTOT = 1280
PARTS = ((0, 128), (128, 256), (384, 384), (768, 384), (1152, 384), (1536, 384))


def permutations():
    by_peer = np.zeros((NLAT, NLAT), np.float32)
    for x in range(NX):
        for y in range(NY):
            for c in range(NC):
                for z in range(NZ):
                    for i in range(2):
                        row = ((x * NZ + z) * NC + c) * 8 + y * 2 + i
                        by_peer[(((x * NY + y) * NC + c) * NZ + z) * 2 + i, row] = 1
    by_z = np.zeros((128, 128), np.float32)
    to_k = np.zeros((128, 256), np.float32)
    for s in range(8):
        for z in range(NZ):
            for i in range(2):
                by_z[z * 16 + i * 8 + s, s * 16 + z * 2 + i] = 1
                to_k[z * 16 + i * 8 + s, i * 64 + z * 8 + s] = 1
                to_k[z * 16 + i * 8 + s, 128 + (1 - i) * 64 + z * 8 + s] = 1
    return tuple(jnp.asarray(a, jnp.bfloat16) for a in (by_peer, by_z, to_k))


def dot(a, b, dims):
    return lax.dot_general(a, b, (dims, ((), ())), preferred_element_type=jnp.float32)


def unit_circle(wave, lon, points):
    inverse = 1.0 / points
    turns = wave * lon
    residue = turns - jnp.floor(turns * inverse) * points
    residue = jnp.where(residue < 0.0, residue + points, residue)
    residue = jnp.where(residue >= points, residue - points, residue)
    folded = jnp.minimum(residue, points - residue)
    u = (points - 4.0 * folded) * ((0.5 * math.pi) * inverse)
    v = u * u
    cosine, sine = jnp.full_like(u, 1.0 / math.factorial(13)), jnp.full_like(u, 1.0 / math.factorial(14))
    for n in range(6):
        cosine = cosine * -v + 1.0 / math.factorial(11 - 2 * n)
        sine = sine * -v + 1.0 / math.factorial(12 - 2 * n)
    sine = 1.0 - v * sine
    cosine = cosine * u
    sine = jnp.where(2.0 * residue <= points, sine, -sine)
    return cosine, sine


def move_kernel(
    m_ref, p_ref, spec_hbm, leg_hbm, by_peer_hbm, by_z_hbm, to_k_hbm,
    a_hbm, b_hbm,
    spec, leg, by_peer, by_z, to_k, coef, sent, mid, ordered, final, a_out,
    waves, cos_now, sin_now, cos_step, sin_step, b_out,
    in_sem, xy_send, xy_recv, xy_own, z_send, z_recv, z_own, a_sem, b_sem,
):
    w, y = lax.axis_index("wave"), lax.axis_index("lev")
    x, z, c = w // 16, lax.rem(w // 2, 8), lax.rem(w, 2)

    def peer(d):
        px, py, pc = lax.rem(x + d // 8, NX), lax.rem(y + lax.rem(d // 2, 4), NY), lax.rem(c + lax.rem(d, 2), NC)
        return px, py, pc

    def wave_of(px, pz, pc):
        return (px * NZ + pz) * NC + pc

    loads = [
        pltpu.make_async_copy(by_peer_hbm, by_peer, in_sem.at[0]),
        pltpu.make_async_copy(by_z_hbm, by_z, in_sem.at[1]),
        pltpu.make_async_copy(to_k_hbm, to_k, in_sem.at[2]),
    ]
    fetch = []
    for g in range(PAIRS):
        cut = pl.ds(2 * g, 2)
        fetch.append((
            pltpu.make_async_copy(spec_hbm.at[cut], spec.at[cut], in_sem.at[3 + 2 * g]),
            pltpu.make_async_copy(leg_hbm.at[cut], leg.at[cut], in_sem.at[4 + 2 * g]),
        ))
    for f in fetch[0]:
        f.start()
    for f in loads:
        f.start()
    for pair in fetch[1:]:
        for f in pair:
            f.start()

    barrier = pltpu.get_barrier_semaphore()

    @pl.loop(1, NPEER)
    def _(d):
        px, py, pc = peer(d)
        pl.semaphore_signal(barrier, inc=1, device_id=(wave_of(px, z, pc), py), device_id_type=MESH)

    @pl.loop(1, NZ)
    def _(d):
        pl.semaphore_signal(barrier, inc=1, device_id=(wave_of(x, lax.rem(z + d, NZ), c), y), device_id_type=MESH)

    for f in loads:
        f.wait()
    slot = y * 8 + x * 2 + c
    own = (x * NY + y) * NC + c

    def spectral(g):
        for f in fetch[g]:
            f.wait()
        for h in range(2):
            r = 2 * g + h
            top = DEG - m_ref[w * WAVES + r]
            degree = lax.broadcasted_iota(jnp.int32, (2 * FL, DEG), 1)
            trimmed = jnp.where(degree < top, spec[r], jnp.zeros((), jnp.bfloat16))
            coef[h * 2 * FL:(h + 1) * 2 * FL, :] = dot(trimmed, leg[r], ((1,), (0,))).astype(jnp.bfloat16)
        moved = dot(by_peer[...], coef[...], ((1,), (1,))).astype(jnp.bfloat16)
        sent[:, :, g * PAIR_LANES:(g + 1) * PAIR_LANES] = moved.reshape(NPEER, 16, PAIR_LANES)

    def send_xy(q):
        first, size = PARTS[q]
        cut = pl.ds(first, size)

        @pl.loop(1, NPEER)
        def _(d):
            px, py, pc = peer(d)
            pltpu.make_async_remote_copy(
                src_ref=sent.at[(px * NY + py) * NC + pc, :, cut],
                dst_ref=mid.at[slot, :, cut],
                send_sem=xy_send.at[q],
                recv_sem=xy_recv.at[q],
                device_id=(wave_of(px, z, pc), py),
                device_id_type=MESH,
            ).start()

        pltpu.make_async_copy(sent.at[own, :, cut], mid.at[slot, :, cut], xy_own.at[q]).start()

    def wait_xy(q):
        first, size = PARTS[q]
        cut = pl.ds(first, size)
        most = mid.at[pl.ds(0, NPEER - 1), :, cut]
        pltpu.make_async_copy(most, most, xy_recv.at[q]).wait()
        pltpu.make_async_copy(sent.at[own, :, cut], mid.at[slot, :, cut], xy_own.at[q]).wait()

    def z_copy(q, d):
        first, size = PARTS[q]
        cut = pl.ds(first, size)
        pz = lax.rem(z + d, NZ)
        return pltpu.make_async_remote_copy(
            src_ref=ordered.at[pz, :, :, cut],
            dst_ref=final.at[z, :, :, cut],
            send_sem=z_send.at[q],
            recv_sem=z_recv.at[q],
            device_id=(wave_of(x, pz, c), y),
            device_id_type=MESH,
        )

    def z_stay(q):
        first, size = PARTS[q]
        cut = pl.ds(first, size)
        return pltpu.make_async_copy(ordered.at[z, :, :, cut], final.at[z, :, :, cut], z_own.at[q])

    def send_z(q):
        first, size = PARTS[q]
        for group in range(NY):
            block = mid[group * 8:(group + 1) * 8, :, first:first + size].reshape(128, size)
            moved = dot(by_z[...], block, ((1,), (0,))).astype(jnp.bfloat16)
            ordered[:, group, :, first:first + size] = moved.reshape(NZ, 16, size)
        for d in (4, 3, 5, 2, 6, 1, 7):
            z_copy(q, d).start()
        z_stay(q).start()

    def wait_z(q):
        first, size = PARTS[q]
        most = final.at[pl.ds(0, NZ - 1), :, :, pl.ds(first, size)]
        pltpu.make_async_copy(most, most, z_recv.at[q]).wait()
        z_stay(q).wait()

    def rows_of(g):
        lane = lax.broadcasted_iota(jnp.int32, (FL, 128), 1)
        for group in range(NY):
            block = final[:, group, :, g * PAIR_LANES:(g + 1) * PAIR_LANES].reshape(128, PAIR_LANES)
            turned = dot(block, to_k[...], ((0,), (0,)))
            for h in range(2):
                real, imag = (turned[(2 * h + k) * FL:(2 * h + k + 1) * FL] for k in range(2))
                even = jnp.where(lane < 64, real[:, :128], imag[:, 128:])
                odd = jnp.where(lane < 64, imag[:, 128:], real[:, :128])
                at = (2 * g + h) * 128
                a_out[0, group * FL:(group + 1) * FL, at:at + 128] = even.astype(jnp.bfloat16)
                a_out[1, group * FL:(group + 1) * FL, at:at + 128] = odd.astype(jnp.bfloat16)

    def a_copy(g):
        cut = pl.ds(g * 256, 256)
        return pltpu.make_async_copy(a_out.at[:, :, cut], a_hbm.at[:, :, cut], a_sem.at[g])

    def b_copy(i, k, t):
        return pltpu.make_async_copy(b_out.at[k], b_hbm.at[i, :, pl.ds(pl.multiple_of(t * 128, 128), 128)], b_sem.at[k])

    def bases():
        @pl.loop(0, KTOT // 2)
        def _(k):
            block, s = k // 64, lax.rem(k, 8)
            source = wave_of(s // 2, lax.rem(k // 8, 8), lax.rem(s, 2))
            waves[pl.ds(k, 1), :] = jnp.full((1, 128), m_ref[source * WAVES + block]).astype(jnp.float32)

        for i in range(2):
            count = p_ref[(w * NY + y) * 2 + i]

            @pl.loop(0, 10)
            def _(block):
                rows = pl.ds(pl.multiple_of(block * 64, 64), 64)
                points = jnp.full((64, 128), count).astype(jnp.float32)
                wave = waves[rows, :]
                lon = lax.broadcasted_iota(jnp.int32, (64, 128), 1).astype(jnp.float32)
                cosine, sine = unit_circle(wave, lon, points)
                weight = jnp.where(2.0 * wave < points, jnp.where(wave == 0.0, 1.0, 2.0), 0.0)
                cos_now[rows, :] = weight * cosine
                sin_now[rows, :] = -weight * sine
                cosine, sine = unit_circle(wave, 128.0, points)
                cos_step[rows, :] = cosine
                sin_step[rows, :] = sine

            @pl.loop(0, TILES)
            def _(t):
                k = lax.rem(t + i * TILES, 2)

                @pl.when(t + i * TILES >= 2)
                def _():
                    b_copy(i, k, t).wait()

                for block in range(10):
                    rows = slice(block * 64, (block + 1) * 64)
                    cosine, sine, cs, ss = cos_now[rows, :], sin_now[rows, :], cos_step[rows, :], sin_step[rows, :]
                    first = block * 128 + i * 64
                    second = block * 128 + (1 - i) * 64
                    b_out[k, first:first + 64, :] = cosine.astype(jnp.bfloat16)
                    b_out[k, second:second + 64, :] = sine.astype(jnp.bfloat16)
                    cos_now[rows, :] = cosine * cs + sine * ss
                    sin_now[rows, :] = sine * cs - cosine * ss
                b_copy(i, k, t).start()

        for k in range(2):
            b_copy(1, k, 0).wait()

    spectral(0)
    pl.semaphore_wait(barrier, NPEER - 1 + NZ - 1)
    send_xy(0)
    send_xy(1)
    for g in range(1, PAIRS):
        spectral(g)
        send_xy(g + 1)
    for q in range(len(PARTS)):
        wait_xy(q)
        send_z(q)
    bases()
    for q in range(len(PARTS)):
        wait_z(q)
        if q:
            rows_of(q - 1)
            a_copy(q - 1).start()
    for g in range(PAIRS):
        a_copy(g).wait()
    for q in range(len(PARTS)):
        first, size = PARTS[q]
        most = mid.at[pl.ds(0, NPEER - 1), :, pl.ds(first, size)]
        pltpu.make_async_copy(most, most, xy_send.at[q]).wait()
        most = final.at[pl.ds(0, NZ - 1), :, :, pl.ds(first, size)]
        pltpu.make_async_copy(most, most, z_send.at[q]).wait()


def move(spectra, legendre_table, m_order, row_points):
    by_peer, by_z, to_k = permutations()
    hbm = pl.BlockSpec(memory_space=pl.ANY)
    smem = pl.BlockSpec(memory_space=pltpu.SMEM)
    n = len(PARTS)
    bf16, f32 = jnp.bfloat16, jnp.float32
    dma = pltpu.SemaphoreType.DMA
    return pl.pallas_call(
        move_kernel,
        out_shape=(
            jax.ShapeDtypeStruct((2, 4 * FL, KTOT), bf16),
            jax.ShapeDtypeStruct((2, KTOT, ROWPAD), bf16),
        ),
        in_specs=[smem, smem, hbm, hbm, hbm, hbm, hbm],
        out_specs=(hbm, hbm),
        scratch_shapes=[
            pltpu.VMEM((WAVES, 2 * FL, DEG), bf16),
            pltpu.VMEM((WAVES, DEG, NLAT), bf16),
            pltpu.VMEM((NLAT, NLAT), bf16),
            pltpu.VMEM((128, 128), bf16),
            pltpu.VMEM((128, 256), bf16),
            pltpu.VMEM((PAIR_LANES, NLAT), bf16),
            pltpu.VMEM((NPEER, 16, LANES), bf16),
            pltpu.VMEM((NPEER, 16, LANES), bf16),
            pltpu.VMEM((NZ, NY, 16, LANES), bf16),
            pltpu.VMEM((NZ, NY, 16, LANES), bf16),
            pltpu.VMEM((2, 4 * FL, KTOT), bf16),
            pltpu.VMEM((KTOT // 2, 128), f32),
            pltpu.VMEM((KTOT // 2, 128), f32),
            pltpu.VMEM((KTOT // 2, 128), f32),
            pltpu.VMEM((KTOT // 2, 128), f32),
            pltpu.VMEM((KTOT // 2, 128), f32),
            pltpu.VMEM((2, KTOT, 128), bf16),
            dma((3 + 2 * PAIRS,)),
            dma((n,)), dma((n,)), dma((n,)),
            dma((n,)), dma((n,)), dma((n,)),
            dma((PAIRS,)), dma((2,)),
        ],
        compiler_params=pltpu.CompilerParams(
            collective_id=0, has_side_effects=True, vmem_limit_bytes=56 << 20
        ),
    )(m_order, row_points, spectra, legendre_table, by_peer, by_z, to_k)


WIDTH = 384


def synth_kernel(p_ref, a_ref, b_ref, grid_ref):
    i, t = pl.program_id(0), pl.program_id(1)
    row = (lax.axis_index("wave") * NY + lax.axis_index("lev")) * 2 + i
    field = dot(a_ref[0], b_ref[0], ((1,), (0,)))
    lon = lax.broadcasted_iota(jnp.int32, (4 * FL, WIDTH), 1) + t * WIDTH
    field = jnp.where(lon < p_ref[row], field, 0.0).astype(jnp.bfloat16)
    for y in range(NY):
        for f in range(3):
            grid_ref[0, f, y * 32:(y + 1) * 32, :] = field[y * FL + f * 32:y * FL + (f + 1) * 32]


def synthesize(a, b, row_points):
    return pl.pallas_call(
        synth_kernel,
        out_shape=jax.ShapeDtypeStruct((2, 3, 128, ROWPAD), jnp.bfloat16),
        grid=(2, ROWPAD // WIDTH),
        in_specs=[
            pl.BlockSpec(memory_space=pltpu.SMEM),
            pl.BlockSpec((1, 4 * FL, KTOT), lambda i, t: (i, 0, 0)),
            pl.BlockSpec((1, KTOT, WIDTH), lambda i, t: (i, 0, t)),
        ],
        out_specs=pl.BlockSpec((1, 3, 128, WIDTH), lambda i, t: (i, 0, 0, t)),
        compiler_params=pltpu.CompilerParams(vmem_limit_bytes=48 << 20),
    )(row_points, a, b)


def shards(spectra, legendre_table, m_order, row_points):
    spectra = spectra.reshape(WAVES, 2 * FL, DEG)
    a, b = move(spectra, legendre_table, m_order, row_points)
    return synthesize(a, b, row_points)


def solution(mesh):
    in_specs = (P("wave", None, None, "lev", None), P("wave", None, None), P(), P())
    out_specs = P(("wave", "lev"), None, None, None)
    return jax.shard_map(shards, mesh=mesh, in_specs=in_specs, out_specs=out_specs, check_vma=False)
```

```python
import functools
import math

import jax
import jax.numpy as jnp
import numpy as np
from jax import lax
from jax.experimental import pallas as pl
from jax.experimental.pallas import tpu as pltpu
from jax.sharding import PartitionSpec as P

MESH = pl.DeviceIdType.MESH
NX, NY, NZ, NC = 4, 4, 8, 2
NPEER = NX * NY * NC
WAVES = 10
PAIRS = WAVES // 2
FL = 96
PAIR_LANES = 4 * FL
LANES = PAIRS * PAIR_LANES
DEG = 640
NLAT = 512
ROWPAD = 2688
TILES = ROWPAD // 128
KTOT = 1280
PARTS = ((0, 128), (128, 256), (384, 384), (768, 384), (1152, 384), (1536, 384))


def permutations():
    by_peer = np.zeros((NLAT, NLAT), np.float32)
    for x in range(NX):
        for y in range(NY):
            for c in range(NC):
                for z in range(NZ):
                    for i in range(2):
                        row = ((x * NZ + z) * NC + c) * 8 + y * 2 + i
                        by_peer[(((x * NY + y) * NC + c) * NZ + z) * 2 + i, row] = 1
    by_z = np.zeros((128, 128), np.float32)
    to_k = np.zeros((128, 256), np.float32)
    for s in range(8):
        for z in range(NZ):
            for i in range(2):
                wave = (s // 2 * NZ + z) * NC + s % 2
                by_z[z * 16 + i * 8 + s, s * 16 + z * 2 + i] = 1
                to_k[z * 16 + i * 8 + s, i * 64 + wave] = 1
                to_k[z * 16 + i * 8 + s, 128 + (1 - i) * 64 + wave] = 1
    return tuple(jnp.asarray(a, jnp.bfloat16) for a in (by_peer, by_z, to_k))


def dot(a, b, dims):
    return lax.dot_general(a, b, (dims, ((), ())), preferred_element_type=jnp.float32)


def unit_circle(wave, lon, points):
    inverse = 1.0 / points
    turns = wave * lon
    residue = turns - jnp.floor(turns * inverse) * points
    residue = jnp.where(residue < 0.0, residue + points, residue)
    residue = jnp.where(residue >= points, residue - points, residue)
    folded = jnp.minimum(residue, points - residue)
    u = (points - 4.0 * folded) * ((0.5 * math.pi) * inverse)
    v = u * u
    cosine, sine = jnp.full_like(u, 1.0 / math.factorial(13)), jnp.full_like(u, 1.0 / math.factorial(14))
    for n in range(6):
        cosine = cosine * -v + 1.0 / math.factorial(11 - 2 * n)
        sine = sine * -v + 1.0 / math.factorial(12 - 2 * n)
    sine = 1.0 - v * sine
    cosine = cosine * u
    sine = jnp.where(2.0 * residue <= points, sine, -sine)
    return cosine, sine


def move_kernel(
    m_ref, p_ref, spec_hbm, leg_hbm, by_peer_hbm, by_z_hbm, to_k_hbm,
    grid_hbm,
    spec, leg, by_peer, by_z, to_k, coef, sent, mid, ordered, final, a_out,
    waves, basis, total, grid,
    in_sem, xy_send, xy_recv, xy_own, z_send, z_recv, z_own, grid_sem,
):
    w, y = lax.axis_index("wave"), lax.axis_index("lev")
    x, z, c = w // 16, lax.rem(w // 2, 8), lax.rem(w, 2)

    def peer(d):
        px, py, pc = lax.rem(x + d // 8, NX), lax.rem(y + lax.rem(d // 2, 4), NY), lax.rem(c + lax.rem(d, 2), NC)
        return px, py, pc

    def wave_of(px, pz, pc):
        return (px * NZ + pz) * NC + pc

    loads = [
        pltpu.make_async_copy(by_peer_hbm, by_peer, in_sem.at[0]),
        pltpu.make_async_copy(by_z_hbm, by_z, in_sem.at[1]),
        pltpu.make_async_copy(to_k_hbm, to_k, in_sem.at[2]),
    ]
    fetch = []
    for g in range(PAIRS):
        cut = pl.ds(2 * g, 2)
        fetch.append((
            pltpu.make_async_copy(spec_hbm.at[cut], spec.at[cut], in_sem.at[3 + 2 * g]),
            pltpu.make_async_copy(leg_hbm.at[cut], leg.at[cut], in_sem.at[4 + 2 * g]),
        ))
    for f in fetch[0]:
        f.start()
    for f in loads:
        f.start()
    for pair in fetch[1:]:
        for f in pair:
            f.start()

    barrier = pltpu.get_barrier_semaphore()

    @pl.loop(1, NPEER)
    def _(d):
        px, py, pc = peer(d)
        pl.semaphore_signal(barrier, inc=1, device_id=(wave_of(px, z, pc), py), device_id_type=MESH)

    @pl.loop(1, NZ)
    def _(d):
        pl.semaphore_signal(barrier, inc=1, device_id=(wave_of(x, lax.rem(z + d, NZ), c), y), device_id_type=MESH)

    for f in loads:
        f.wait()
    slot = y * 8 + x * 2 + c
    own = (x * NY + y) * NC + c

    def spectral(g):
        for f in fetch[g]:
            f.wait()
        for h in range(2):
            r = 2 * g + h
            top = DEG - m_ref[w * WAVES + r]
            degree = lax.broadcasted_iota(jnp.int32, (2 * FL, DEG), 1)
            trimmed = jnp.where(degree < top, spec[r], jnp.zeros((), jnp.bfloat16))
            coef[h * 2 * FL:(h + 1) * 2 * FL, :] = dot(trimmed, leg[r], ((1,), (0,))).astype(jnp.bfloat16)
        moved = dot(by_peer[...], coef[...], ((1,), (1,))).astype(jnp.bfloat16)
        sent[:, :, g * PAIR_LANES:(g + 1) * PAIR_LANES] = moved.reshape(NPEER, 16, PAIR_LANES)

    def send_xy(q):
        first, size = PARTS[q]
        cut = pl.ds(first, size)

        @pl.loop(1, NPEER)
        def _(d):
            px, py, pc = peer(d)
            pltpu.make_async_remote_copy(
                src_ref=sent.at[(px * NY + py) * NC + pc, :, cut],
                dst_ref=mid.at[slot, :, cut],
                send_sem=xy_send.at[q],
                recv_sem=xy_recv.at[q],
                device_id=(wave_of(px, z, pc), py),
                device_id_type=MESH,
            ).start()

        pltpu.make_async_copy(sent.at[own, :, cut], mid.at[slot, :, cut], xy_own.at[q]).start()

    def wait_xy(q):
        first, size = PARTS[q]
        cut = pl.ds(first, size)
        most = mid.at[pl.ds(0, NPEER - 1), :, cut]
        pltpu.make_async_copy(most, most, xy_recv.at[q]).wait()
        pltpu.make_async_copy(sent.at[own, :, cut], mid.at[slot, :, cut], xy_own.at[q]).wait()

    def z_copy(q, d):
        first, size = PARTS[q]
        cut = pl.ds(first, size)
        pz = lax.rem(z + d, NZ)
        return pltpu.make_async_remote_copy(
            src_ref=ordered.at[pz, :, :, cut],
            dst_ref=final.at[z, :, :, cut],
            send_sem=z_send.at[q],
            recv_sem=z_recv.at[q],
            device_id=(wave_of(x, pz, c), y),
            device_id_type=MESH,
        )

    def z_stay(q):
        first, size = PARTS[q]
        cut = pl.ds(first, size)
        return pltpu.make_async_copy(ordered.at[z, :, :, cut], final.at[z, :, :, cut], z_own.at[q])

    def send_z(q):
        first, size = PARTS[q]
        for group in range(NY):
            block = mid[group * 8:(group + 1) * 8, :, first:first + size].reshape(128, size)
            moved = dot(by_z[...], block, ((1,), (0,))).astype(jnp.bfloat16)
            ordered[:, group, :, first:first + size] = moved.reshape(NZ, 16, size)
        for d in (4, 3, 5, 2, 6, 1, 7):
            z_copy(q, d).start()
        z_stay(q).start()

    def wait_z(q):
        first, size = PARTS[q]
        most = final.at[pl.ds(0, NZ - 1), :, :, pl.ds(first, size)]
        pltpu.make_async_copy(most, most, z_recv.at[q]).wait()
        z_stay(q).wait()

    def rows_of(g):
        lane = lax.broadcasted_iota(jnp.int32, (FL, 128), 1)
        for group in range(NY):
            block = final[:, group, :, g * PAIR_LANES:(g + 1) * PAIR_LANES].reshape(128, PAIR_LANES)
            turned = dot(block, to_k[...], ((0,), (0,)))
            for h in range(2):
                real, imag = (turned[(2 * h + k) * FL:(2 * h + k + 1) * FL] for k in range(2))
                even = jnp.where(lane < 64, real[:, :128], imag[:, 128:])
                odd = jnp.where(lane < 64, imag[:, 128:], real[:, :128])
                at = (2 * g + h) * 128
                a_out[0, group * FL:(group + 1) * FL, at:at + 128] = even.astype(jnp.bfloat16)
                a_out[1, group * FL:(group + 1) * FL, at:at + 128] = odd.astype(jnp.bfloat16)

    def gather_waves():
        @pl.loop(0, KTOT // 2 // WAVES)
        def _(k):
            for block in range(WAVES):
                waves[pl.ds(block * 64 + k, 1), :] = jnp.full((1, 128), m_ref[k * WAVES + block]).astype(jnp.float32)

    def make_basis(i, block):
        points = jnp.full((64, 128), p_ref[(w * NY + y) * 2 + i]).astype(jnp.float32)
        wave = waves[block * 64:(block + 1) * 64, :]
        lon = lax.broadcasted_iota(jnp.int32, (64, 128), 1).astype(jnp.float32)
        weight = jnp.where(2.0 * wave < points, jnp.where(wave == 0.0, 1.0, 2.0), 0.0)
        cosine, sine = unit_circle(wave, lon, points)
        cos_step, sin_step = unit_circle(wave, 128.0, points)
        first = block * 128 + i * 64
        second = block * 128 + (1 - i) * 64

        def step(t, now):
            cosine, sine = now
            cut = pl.ds(pl.multiple_of(t * 128, 128), 128)
            basis[i, first:first + 64, cut] = cosine.astype(jnp.bfloat16)
            basis[i, second:second + 64, cut] = sine.astype(jnp.bfloat16)
            return cosine * cos_step + sine * sin_step, sine * cos_step - cosine * sin_step

        lax.fori_loop(0, TILES, step, (weight * cosine, -weight * sine))

    def bases(lo, hi):
        for n in range(lo, hi):
            make_basis(n % 2, n // 2)

    def multiply(g):
        k = slice(g * 256, (g + 1) * 256)
        for i in range(2):
            def part(cut):
                total[i, :, cut] = dot(a_out[i, :, k], basis[i, k, cut], ((1,), (0,))) + (total[i, :, cut] if g else 0.0)

            @pl.loop(0, 5)
            def _(t):
                part(pl.ds(pl.multiple_of(t * 512, 512), 512))

            part(pl.ds(2560, 128))

    def grid_copy(i, t):
        cut = pl.ds(t * 384, 384)
        return pltpu.make_async_copy(grid.at[i, :, :, cut], grid_hbm.at[i, :, :, cut], grid_sem.at[i * 7 + t])

    def finish(g):
        k = slice(g * 256, (g + 1) * 256)
        for i in range(2):
            points = p_ref[(w * NY + y) * 2 + i]
            for t in range(7):
                cut = slice(t * 384, (t + 1) * 384)
                field = dot(a_out[i, :, k], basis[i, k, cut], ((1,), (0,))) + total[i, :, cut]
                lon = lax.broadcasted_iota(jnp.int32, (4 * FL, 384), 1) + t * 384
                field = jnp.where(lon < points, field, 0.0).astype(jnp.bfloat16)
                for group in range(NY):
                    for f in range(3):
                        at = group * FL + f * 32
                        grid[i, f, group * 32:(group + 1) * 32, cut] = field[at:at + 32]
                grid_copy(i, t).start()

    spectral(0)
    pl.semaphore_wait(barrier, NPEER - 1 + NZ - 1)
    send_xy(0)
    send_xy(1)
    spectral(1)
    send_xy(2)
    wait_xy(0)
    send_z(0)
    spectral(2)
    send_xy(3)
    wait_xy(1)
    send_z(1)
    spectral(3)
    send_xy(4)
    spectral(4)
    send_xy(5)
    gather_waves()
    bases(0, 4)
    wait_xy(2)
    send_z(2)
    bases(4, 8)
    wait_xy(3)
    send_z(3)
    bases(8, 14)
    wait_xy(4)
    send_z(4)
    bases(14, 20)
    wait_xy(5)
    send_z(5)
    wait_z(0)
    for g in range(PAIRS):
        wait_z(g + 1)
        rows_of(g)
        if g < PAIRS - 1:
            multiply(g)
    finish(PAIRS - 1)
    for q in range(len(PARTS)):
        first, size = PARTS[q]
        most = mid.at[pl.ds(0, NPEER - 1), :, pl.ds(first, size)]
        pltpu.make_async_copy(most, most, xy_send.at[q]).wait()
        most = final.at[pl.ds(0, NZ - 1), :, :, pl.ds(first, size)]
        pltpu.make_async_copy(most, most, z_send.at[q]).wait()
    for i in range(2):
        for t in range(7):
            grid_copy(i, t).wait()


def move(spectra, legendre_table, m_order, row_points):
    by_peer, by_z, to_k = permutations()
    hbm = pl.BlockSpec(memory_space=pl.ANY)
    smem = pl.BlockSpec(memory_space=pltpu.SMEM)
    n = len(PARTS)
    bf16, f32 = jnp.bfloat16, jnp.float32
    dma = pltpu.SemaphoreType.DMA
    return pl.pallas_call(
        move_kernel,
        out_shape=jax.ShapeDtypeStruct((2, 3, 128, ROWPAD), bf16),
        in_specs=[smem, smem, hbm, hbm, hbm, hbm, hbm],
        out_specs=hbm,
        scratch_shapes=[
            pltpu.VMEM((WAVES, 2 * FL, DEG), bf16),
            pltpu.VMEM((WAVES, DEG, NLAT), bf16),
            pltpu.VMEM((NLAT, NLAT), bf16),
            pltpu.VMEM((128, 128), bf16),
            pltpu.VMEM((128, 256), bf16),
            pltpu.VMEM((PAIR_LANES, NLAT), bf16),
            pltpu.VMEM((NPEER, 16, LANES), bf16),
            pltpu.VMEM((NPEER, 16, LANES), bf16),
            pltpu.VMEM((NZ, NY, 16, LANES), bf16),
            pltpu.VMEM((NZ, NY, 16, LANES), bf16),
            pltpu.VMEM((2, 4 * FL, KTOT), bf16),
            pltpu.VMEM((KTOT // 2, 128), f32),
            pltpu.VMEM((2, KTOT, ROWPAD), bf16),
            pltpu.VMEM((2, 4 * FL, ROWPAD), f32),
            pltpu.VMEM((2, 3, 128, ROWPAD), bf16),
            dma((3 + 2 * PAIRS,)),
            dma((n,)), dma((n,)), dma((n,)),
            dma((n,)), dma((n,)), dma((n,)),
            dma((14,)),
        ],
        compiler_params=pltpu.CompilerParams(
            collective_id=0, has_side_effects=True, vmem_limit_bytes=56 << 20
        ),
    )(m_order, row_points, spectra, legendre_table, by_peer, by_z, to_k)


def shards(spectra, legendre_table, m_order, row_points):
    spectra = spectra.reshape(WAVES, 2 * FL, DEG)
    return move(spectra, legendre_table, m_order, row_points)


def solution(mesh):
    in_specs = (P("wave", None, None, "lev", None), P("wave", None, None), P(), P())
    out_specs = P(("wave", "lev"), None, None, None)
    return jax.shard_map(shards, mesh=mesh, in_specs=in_specs, out_specs=out_specs, check_vma=False)
```

```python
import functools
import math

import jax
import jax.numpy as jnp
import numpy as np
from jax import lax
from jax.experimental import pallas as pl
from jax.experimental.pallas import tpu as pltpu
from jax.sharding import PartitionSpec as P

MESH = pl.DeviceIdType.MESH
NX, NY, NZ, NC = 4, 4, 8, 2
NPEER = NX * NY * NC
WAVES = 10
PAIRS = WAVES // 2
FL = 96
PAIR_LANES = 4 * FL
LANES = PAIRS * PAIR_LANES
DEG = 640
NLAT = 512
ROWPAD = 2688
TILES = ROWPAD // 128
KTOT = 1280
PARTS = ((0, 384), (384, 128), (512, 256), (768, 384), (1152, 384), (1536, 384))


def permutations():
    by_peer = np.zeros((NLAT, NLAT), np.float32)
    for x in range(NX):
        for y in range(NY):
            for c in range(NC):
                for z in range(NZ):
                    for i in range(2):
                        row = ((x * NZ + z) * NC + c) * 8 + y * 2 + i
                        by_peer[(((x * NY + y) * NC + c) * NZ + z) * 2 + i, row] = 1
    by_z = np.zeros((128, 128), np.float32)
    to_k = np.zeros((128, 256), np.float32)
    for s in range(8):
        for z in range(NZ):
            for i in range(2):
                wave = (s // 2 * NZ + z) * NC + s % 2
                by_z[z * 16 + i * 8 + s, s * 16 + z * 2 + i] = 1
                to_k[z * 16 + i * 8 + s, i * 64 + wave] = 1
                to_k[z * 16 + i * 8 + s, 128 + (1 - i) * 64 + wave] = 1
    return tuple(jnp.asarray(a, jnp.bfloat16) for a in (by_peer, by_z, to_k))


def dot(a, b, dims):
    return lax.dot_general(a, b, (dims, ((), ())), preferred_element_type=jnp.float32)


def unit_circle(wave, lon, points):
    inverse = 1.0 / points
    turns = wave * lon
    residue = turns - jnp.floor(turns * inverse) * points
    residue = jnp.where(residue < 0.0, residue + points, residue)
    residue = jnp.where(residue >= points, residue - points, residue)
    folded = jnp.minimum(residue, points - residue)
    u = (points - 4.0 * folded) * ((0.5 * math.pi) * inverse)
    v = u * u
    cosine, sine = jnp.full_like(u, 1.0 / math.factorial(13)), jnp.full_like(u, 1.0 / math.factorial(14))
    for n in range(6):
        cosine = cosine * -v + 1.0 / math.factorial(11 - 2 * n)
        sine = sine * -v + 1.0 / math.factorial(12 - 2 * n)
    sine = 1.0 - v * sine
    cosine = cosine * u
    sine = jnp.where(2.0 * residue <= points, sine, -sine)
    return cosine, sine


def move_kernel(
    m_ref, p_ref, spec_hbm, leg_hbm, by_peer_hbm, by_z_hbm, to_k_hbm,
    total, a_last, basis_last,
    spec, leg, by_peer, by_z, to_k, coef, sent, mid, ordered, final, a_now,
    waves, basis,
    in_sem, xy_send, xy_recv, xy_own, z_send, z_recv, z_own,
):
    w, y = lax.axis_index("wave"), lax.axis_index("lev")
    x, z, c = w // 16, lax.rem(w // 2, 8), lax.rem(w, 2)

    ys = [lax.rem(y + d, NY) for d in range(NY)]

    def each_peer(act):
        @pl.loop(0, NX)
        def _(d):
            px = lax.rem(x + d, NX)

            @pl.when(d > 0)
            def _():
                act(px, y, c)

            for py in ys[1:]:
                act(px, py, c)
            for py in ys:
                act(px, py, 1 - c)

    def wave_of(px, pz, pc):
        return (px * NZ + pz) * NC + pc

    loads = [
        pltpu.make_async_copy(by_peer_hbm, by_peer, in_sem.at[0]),
        pltpu.make_async_copy(by_z_hbm, by_z, in_sem.at[1]),
        pltpu.make_async_copy(to_k_hbm, to_k, in_sem.at[2]),
    ]
    fetch = []
    for g in range(PAIRS):
        cut = pl.ds(2 * g, 2)
        fetch.append((
            pltpu.make_async_copy(spec_hbm.at[cut], spec.at[cut], in_sem.at[3 + 2 * g]),
            pltpu.make_async_copy(leg_hbm.at[cut], leg.at[cut], in_sem.at[4 + 2 * g]),
        ))
    for f in fetch[0]:
        f.start()
    for f in loads:
        f.start()
    for pair in fetch[1:]:
        for f in pair:
            f.start()

    barrier = pltpu.get_barrier_semaphore()

    def greet(px, py, pc):
        pl.semaphore_signal(barrier, inc=1, device_id=(wave_of(px, z, pc), py), device_id_type=MESH)

    each_peer(greet)

    @pl.loop(1, NZ)
    def _(d):
        pl.semaphore_signal(barrier, inc=1, device_id=(wave_of(x, lax.rem(z + d, NZ), c), y), device_id_type=MESH)

    for f in loads:
        f.wait()
    slot = y * 8 + x * 2 + c
    own = (x * NY + y) * NC + c

    def spectral(g):
        for f in fetch[g]:
            f.wait()
        for h in range(2):
            r = 2 * g + h
            top = DEG - m_ref[w * WAVES + r]
            degree = lax.broadcasted_iota(jnp.int32, (2 * FL, DEG), 1)
            trimmed = jnp.where(degree < top, spec[r], jnp.zeros((), jnp.bfloat16))
            coef[h * 2 * FL:(h + 1) * 2 * FL, :] = dot(trimmed, leg[r], ((1,), (0,))).astype(jnp.bfloat16)
        moved = dot(by_peer[...], coef[...], ((1,), (1,))).astype(jnp.bfloat16)
        sent[:, :, g * PAIR_LANES:(g + 1) * PAIR_LANES] = moved.reshape(NPEER, 16, PAIR_LANES)

    def send_xy(q):
        first, size = PARTS[q]
        cut = pl.ds(first, size)

        def send(px, py, pc):
            pltpu.make_async_remote_copy(
                src_ref=sent.at[(px * NY + py) * NC + pc, :, cut],
                dst_ref=mid.at[slot, :, cut],
                send_sem=xy_send.at[q],
                recv_sem=xy_recv.at[q],
                device_id=(wave_of(px, z, pc), py),
                device_id_type=MESH,
            ).start()

        each_peer(send)
        pltpu.make_async_copy(sent.at[own, :, cut], mid.at[slot, :, cut], xy_own.at[q]).start()

    def wait_xy(q):
        first, size = PARTS[q]
        cut = pl.ds(first, size)
        most = mid.at[pl.ds(0, NPEER - 1), :, cut]
        pltpu.make_async_copy(most, most, xy_recv.at[q]).wait()
        pltpu.make_async_copy(sent.at[own, :, cut], mid.at[slot, :, cut], xy_own.at[q]).wait()

    def z_copy(q, d):
        first, size = PARTS[q]
        cut = pl.ds(first, size)
        pz = lax.rem(z + d, NZ)
        return pltpu.make_async_remote_copy(
            src_ref=ordered.at[pz, :, :, cut],
            dst_ref=final.at[z, :, :, cut],
            send_sem=z_send.at[q],
            recv_sem=z_recv.at[q],
            device_id=(wave_of(x, pz, c), y),
            device_id_type=MESH,
        )

    def z_stay(q):
        first, size = PARTS[q]
        cut = pl.ds(first, size)
        return pltpu.make_async_copy(ordered.at[z, :, :, cut], final.at[z, :, :, cut], z_own.at[q])

    def order_z(q, rows):
        first, size = PARTS[q]
        for group in range(NY):
            block = rows[group * 8:(group + 1) * 8, :, first:first + size].reshape(128, size)
            moved = dot(by_z[...], block, ((1,), (0,))).astype(jnp.bfloat16)
            ordered[:, group, :, first:first + size] = moved.reshape(NZ, 16, size)

    def send_z(q):
        for d in (4, 3, 5, 2, 6, 1, 7):
            z_copy(q, d).start()
        z_stay(q).start()

    def wait_z(q):
        first, size = PARTS[q]
        most = final.at[pl.ds(0, NZ - 1), :, :, pl.ds(first, size)]
        pltpu.make_async_copy(most, most, z_recv.at[q]).wait()
        z_stay(q).wait()

    def order_xy(q):
        first, size = PARTS[q]
        for px in range(NX):
            block = final[:, px, :, first:first + size].reshape(128, size)
            moved = dot(by_z[...], block, ((0,), (0,))).astype(jnp.bfloat16)
            sent[px * 8:(px + 1) * 8, :, first:first + size] = moved.reshape(8, 16, size)

    def rows_of(g):
        lane = lax.broadcasted_iota(jnp.int32, (FL, 128), 1)
        for group in range(NY):
            if g == 0:
                block = mid[group * 8:(group + 1) * 8, :, :PAIR_LANES].reshape(128, PAIR_LANES)
                block = dot(by_z[...], block, ((1,), (0,))).astype(jnp.bfloat16)
            else:
                block = final[:, group, :, g * PAIR_LANES:(g + 1) * PAIR_LANES].reshape(128, PAIR_LANES)
            turned = dot(block, to_k[...], ((0,), (0,)))
            for h in range(2):
                real, imag = (turned[(2 * h + k) * FL:(2 * h + k + 1) * FL] for k in range(2))
                even = jnp.where(lane < 64, real[:, :128], imag[:, 128:])
                odd = jnp.where(lane < 64, imag[:, 128:], real[:, :128])
                to = a_last if g == PAIRS - 1 else a_now
                to[0, group * FL:(group + 1) * FL, h * 128:(h + 1) * 128] = even.astype(jnp.bfloat16)
                to[1, group * FL:(group + 1) * FL, h * 128:(h + 1) * 128] = odd.astype(jnp.bfloat16)

    def gather_waves():
        @pl.loop(0, KTOT // 2 // WAVES)
        def _(k):
            for block in range(WAVES):
                waves[pl.ds(block * 64 + k, 1), :] = jnp.full((1, 128), m_ref[k * WAVES + block]).astype(jnp.float32)

    def make_basis(i, block):
        points = jnp.full((64, 128), p_ref[(w * NY + y) * 2 + i]).astype(jnp.float32)
        wave = waves[block * 64:(block + 1) * 64, :]
        lon = lax.broadcasted_iota(jnp.int32, (64, 128), 1).astype(jnp.float32)
        weight = jnp.where(2.0 * wave < points, jnp.where(wave == 0.0, 1.0, 2.0), 0.0)
        cosine, sine = unit_circle(wave, lon, points)
        cos_step, sin_step = unit_circle(wave, 128.0, points)
        to, at = (basis_last, block - 8) if block >= 8 else (basis, block)
        first = at * 128 + i * 64
        second = at * 128 + (1 - i) * 64

        def step(t, now):
            cosine, sine = now
            cut = pl.ds(pl.multiple_of(t * 128, 128), 128)
            to[i, first:first + 64, cut] = cosine.astype(jnp.bfloat16)
            to[i, second:second + 64, cut] = sine.astype(jnp.bfloat16)
            return cosine * cos_step + sine * sin_step, sine * cos_step - cosine * sin_step

        lax.fori_loop(0, TILES, step, (weight * cosine, -weight * sine))

    def bases(lo, hi):
        for n in range(lo, hi):
            make_basis(n % 2, n // 2)

    def multiply(g):
        k = slice(g * 256, (g + 1) * 256)
        for i in range(2):
            def part(cut):
                total[i, :, cut] = dot(a_now[i], basis[i, k, cut], ((1,), (0,))) + (total[i, :, cut] if g else 0.0)

            @pl.loop(0, 5)
            def _(t):
                part(pl.ds(pl.multiple_of(t * 512, 512), 512))

            part(pl.ds(2560, 128))

    def pass_on(q):
        wait_xy(q)
        order_z(q, mid)
        send_z(q)

    spectral(0)
    order_z(0, sent)
    pl.semaphore_wait(barrier, NPEER - 1 + NZ - 1)
    send_z(0)
    spectral(1)
    send_xy(1)
    send_xy(2)
    spectral(2)
    send_xy(3)
    pass_on(1)
    spectral(3)
    send_xy(4)
    pass_on(2)
    spectral(4)
    send_xy(5)
    wait_z(0)
    order_xy(0)
    send_xy(0)
    gather_waves()
    bases(0, 4)
    pass_on(3)
    bases(4, 10)
    pass_on(4)
    bases(10, 16)
    pass_on(5)
    bases(16, 20)
    wait_xy(0)
    rows_of(0)
    multiply(0)
    wait_z(1)
    wait_z(2)
    rows_of(1)
    multiply(1)
    for g in range(2, PAIRS):
        wait_z(g + 1)
        rows_of(g)
        if g < PAIRS - 1:
            multiply(g)
    for q in range(len(PARTS)):
        first, size = PARTS[q]
        most = mid.at[pl.ds(0, NPEER - 1), :, pl.ds(first, size)]
        pltpu.make_async_copy(most, most, xy_send.at[q]).wait()
        most = final.at[pl.ds(0, NZ - 1), :, :, pl.ds(first, size)]
        pltpu.make_async_copy(most, most, z_send.at[q]).wait()


def move(spectra, legendre_table, m_order, row_points):
    by_peer, by_z, to_k = permutations()
    hbm = pl.BlockSpec(memory_space=pl.ANY)
    smem = pl.BlockSpec(memory_space=pltpu.SMEM)
    n = len(PARTS)
    bf16, f32 = jnp.bfloat16, jnp.float32
    dma = pltpu.SemaphoreType.DMA
    return pl.pallas_call(
        move_kernel,
        out_shape=(
            pltpu.VMEM((2, 4 * FL, ROWPAD), f32),
            pltpu.VMEM((2, 4 * FL, 256), bf16),
            pltpu.VMEM((2, 256, ROWPAD), bf16),
        ),
        in_specs=[smem, smem, hbm, hbm, hbm, hbm, hbm],
        out_specs=(pl.BlockSpec(memory_space=pltpu.VMEM),) * 3,
        scratch_shapes=[
            pltpu.VMEM((WAVES, 2 * FL, DEG), bf16),
            pltpu.VMEM((WAVES, DEG, NLAT), bf16),
            pltpu.VMEM((NLAT, NLAT), bf16),
            pltpu.VMEM((128, 128), bf16),
            pltpu.VMEM((128, 256), bf16),
            pltpu.VMEM((PAIR_LANES, NLAT), bf16),
            pltpu.VMEM((NPEER, 16, LANES), bf16),
            pltpu.VMEM((NPEER, 16, LANES), bf16),
            pltpu.VMEM((NZ, NY, 16, LANES), bf16),
            pltpu.VMEM((NZ, NY, 16, LANES), bf16),
            pltpu.VMEM((2, 4 * FL, 256), bf16),
            pltpu.VMEM((KTOT // 2, 128), f32),
            pltpu.VMEM((2, KTOT - 256, ROWPAD), bf16),
            dma((3 + 2 * PAIRS,)),
            dma((n,)), dma((n,)), dma((n,)),
            dma((n,)), dma((n,)), dma((n,)),
        ],
        compiler_params=pltpu.CompilerParams(
            collective_id=0, has_side_effects=True, vmem_limit_bytes=51 << 20
        ),
    )(m_order, row_points, spectra, legendre_table, by_peer, by_z, to_k)


CUT = 384
CUTS = ROWPAD // CUT


def finish_kernel(p_ref, total, a_last, basis_last, grid_hbm, grid, grid_sem):
    row = (lax.axis_index("wave") * NY + lax.axis_index("lev")) * 2
    copies = []
    for i in range(2):
        points = p_ref[row + i]
        for t in range(CUTS):
            cut = slice(t * CUT, (t + 1) * CUT)
            field = dot(a_last[i], basis_last[i, :, cut], ((1,), (0,))) + total[i, :, cut]
            lon = lax.broadcasted_iota(jnp.int32, (4 * FL, CUT), 1) + t * CUT
            field = jnp.where(lon < points, field, 0.0).astype(jnp.bfloat16)
            for y in range(NY):
                for f in range(3):
                    grid[i, f, y * 32:(y + 1) * 32, cut] = field[y * FL + f * 32:y * FL + (f + 1) * 32]
            cut = pl.ds(t * CUT, CUT)
            copy = pltpu.make_async_copy(grid.at[i, :, :, cut], grid_hbm.at[i, :, :, cut], grid_sem.at[i * CUTS + t])
            copy.start()
            copies.append(copy)
    for copy in copies:
        copy.wait()


def finish(total, a_last, basis_last, row_points):
    held = pl.BlockSpec(memory_space=pltpu.VMEM)
    return pl.pallas_call(
        finish_kernel,
        out_shape=jax.ShapeDtypeStruct((2, 3, 128, ROWPAD), jnp.bfloat16),
        in_specs=[pl.BlockSpec(memory_space=pltpu.SMEM), held, held, held],
        out_specs=pl.BlockSpec(memory_space=pl.ANY),
        scratch_shapes=[
            pltpu.VMEM((2, 3, 128, ROWPAD), jnp.bfloat16),
            pltpu.SemaphoreType.DMA((2 * CUTS,)),
        ],
        compiler_params=pltpu.CompilerParams(vmem_limit_bytes=12 << 20),
    )(row_points, *(pltpu.with_memory_space_constraint(v, pltpu.VMEM) for v in (total, a_last, basis_last)))


def shards(spectra, legendre_table, m_order, row_points):
    spectra = spectra.reshape(WAVES, 2 * FL, DEG)
    held = move(spectra, legendre_table, m_order, row_points)
    return finish(*held, row_points)


def solution(mesh):
    in_specs = (P("wave", None, None, "lev", None), P("wave", None, None), P(), P())
    out_specs = P(("wave", "lev"), None, None, None)
    return jax.shard_map(shards, mesh=mesh, in_specs=in_specs, out_specs=out_specs, check_vma=False)
```

```python
import functools
import math

import jax
import jax.numpy as jnp
import numpy as np
from jax import lax
from jax.experimental import pallas as pl
from jax.experimental.pallas import tpu as pltpu
from jax.sharding import PartitionSpec as P

MESH = pl.DeviceIdType.MESH
NX, NY, NZ, NC = 4, 4, 8, 2
NPEER = NX * NY * NC
WAVES = 10
PAIRS = WAVES // 2
FL = 96
PAIR_LANES = 4 * FL
LANES = PAIRS * PAIR_LANES
DEG = 640
NLAT = 512
ROWPAD = 2688
TILES = ROWPAD // 128
KTOT = 1280
PARTS = ((0, 384), (384, 128), (512, 256), (768, 384), (1152, 384), (1536, 384))


def permutations():
    by_peer = np.zeros((NLAT, NLAT), np.float32)
    for x in range(NX):
        for y in range(NY):
            for c in range(NC):
                for z in range(NZ):
                    for i in range(2):
                        row = ((x * NZ + z) * NC + c) * 8 + y * 2 + i
                        by_peer[(((x * NY + y) * NC + c) * NZ + z) * 2 + i, row] = 1
    by_z = np.zeros((128, 128), np.float32)
    to_k = np.zeros((128, 256), np.float32)
    for s in range(8):
        for z in range(NZ):
            for i in range(2):
                wave = (s // 2 * NZ + z) * NC + s % 2
                by_z[z * 16 + i * 8 + s, s * 16 + z * 2 + i] = 1
                to_k[z * 16 + i * 8 + s, i * 64 + wave] = 1
                to_k[z * 16 + i * 8 + s, 128 + (1 - i) * 64 + wave] = 1
    return tuple(jnp.asarray(a, jnp.bfloat16) for a in (by_peer, by_z, to_k))


def dot(a, b, dims):
    return lax.dot_general(a, b, (dims, ((), ())), preferred_element_type=jnp.float32)


def unit_circle(wave, lon, points):
    inverse = 1.0 / points
    turns = wave * lon
    residue = turns - jnp.floor(turns * inverse) * points
    residue = jnp.where(residue < 0.0, residue + points, residue)
    residue = jnp.where(residue >= points, residue - points, residue)
    folded = jnp.minimum(residue, points - residue)
    u = (points - 4.0 * folded) * ((0.5 * math.pi) * inverse)
    v = u * u
    cosine, sine = jnp.full_like(u, 1.0 / math.factorial(13)), jnp.full_like(u, 1.0 / math.factorial(14))
    for n in range(6):
        cosine = cosine * -v + 1.0 / math.factorial(11 - 2 * n)
        sine = sine * -v + 1.0 / math.factorial(12 - 2 * n)
    sine = 1.0 - v * sine
    cosine = cosine * u
    sine = jnp.where(2.0 * residue <= points, sine, -sine)
    return cosine, sine


def move_kernel(
    m_ref, p_ref, spec_hbm, leg_hbm, by_peer_hbm, by_z_hbm, to_k_hbm,
    total, a_last, basis_last,
    spec, leg, by_peer, by_z, to_k, coef, sent, mid, ordered, final, a_now,
    waves, basis,
    in_sem, xy_send, xy_recv, xy_own, z_send, z_recv, z_own,
):
    w, y = lax.axis_index("wave"), lax.axis_index("lev")
    x, z, c = w // 16, lax.rem(w // 2, 8), lax.rem(w, 2)

    ys = [lax.rem(y + d, NY) for d in range(NY)]

    def each_peer(act):
        @pl.loop(0, NX)
        def _(d):
            px = lax.rem(x + d, NX)

            @pl.when(d > 0)
            def _():
                act(px, y, c)

            for py in ys[1:]:
                act(px, py, c)
            for py in ys:
                act(px, py, 1 - c)

    def wave_of(px, pz, pc):
        return (px * NZ + pz) * NC + pc

    loads = [
        pltpu.make_async_copy(by_peer_hbm, by_peer, in_sem.at[0]),
        pltpu.make_async_copy(by_z_hbm, by_z, in_sem.at[1]),
        pltpu.make_async_copy(to_k_hbm, to_k, in_sem.at[2]),
    ]
    fetch = []
    for g in range(PAIRS):
        cut = pl.ds(2 * g, 2)
        fetch.append((
            pltpu.make_async_copy(spec_hbm.at[cut], spec.at[cut], in_sem.at[3 + 2 * g]),
            pltpu.make_async_copy(leg_hbm.at[cut], leg.at[cut], in_sem.at[4 + 2 * g]),
        ))
    for f in (*fetch[0], *loads[:2]):
        f.start()

    barrier = pltpu.get_barrier_semaphore()

    @pl.loop(1, NZ)
    def _(d):
        pl.semaphore_signal(barrier, inc=1, device_id=(wave_of(x, lax.rem(z + d, NZ), c), y), device_id_type=MESH)

    def greet(px, py, pc):
        pl.semaphore_signal(barrier, inc=1, device_id=(wave_of(px, z, pc), py), device_id_type=MESH)

    each_peer(greet)
    for f in (*sum(fetch[1:], ()), loads[2]):
        f.start()
    for f in loads[:2]:
        f.wait()
    slot = y * 8 + x * 2 + c
    own = (x * NY + y) * NC + c

    def spectral(g):
        for f in fetch[g]:
            f.wait()
        for h in range(2):
            r = 2 * g + h
            top = DEG - m_ref[w * WAVES + r]
            degree = lax.broadcasted_iota(jnp.int32, (2 * FL, DEG), 1)
            trimmed = jnp.where(degree < top, spec[r], jnp.zeros((), jnp.bfloat16))
            coef[h * 2 * FL:(h + 1) * 2 * FL, :] = dot(trimmed, leg[r], ((1,), (0,))).astype(jnp.bfloat16)
        moved = dot(by_peer[...], coef[...], ((1,), (1,))).astype(jnp.bfloat16)
        sent[:, :, g * PAIR_LANES:(g + 1) * PAIR_LANES] = moved.reshape(NPEER, 16, PAIR_LANES)

    def send_xy(q):
        first, size = PARTS[q]
        cut = pl.ds(first, size)

        def send(px, py, pc):
            pltpu.make_async_remote_copy(
                src_ref=sent.at[(px * NY + py) * NC + pc, :, cut],
                dst_ref=mid.at[slot, :, cut],
                send_sem=xy_send.at[q],
                recv_sem=xy_recv.at[q],
                device_id=(wave_of(px, z, pc), py),
                device_id_type=MESH,
            ).start()

        each_peer(send)
        pltpu.make_async_copy(sent.at[own, :, cut], mid.at[slot, :, cut], xy_own.at[q]).start()

    def wait_xy(q):
        first, size = PARTS[q]
        cut = pl.ds(first, size)
        most = mid.at[pl.ds(0, NPEER - 1), :, cut]
        pltpu.make_async_copy(most, most, xy_recv.at[q]).wait()
        pltpu.make_async_copy(sent.at[own, :, cut], mid.at[slot, :, cut], xy_own.at[q]).wait()

    def z_copy(q, d):
        first, size = PARTS[q]
        cut = pl.ds(first, size)
        pz = lax.rem(z + d, NZ)
        return pltpu.make_async_remote_copy(
            src_ref=ordered.at[pz, :, :, cut],
            dst_ref=final.at[z, :, :, cut],
            send_sem=z_send.at[q],
            recv_sem=z_recv.at[q],
            device_id=(wave_of(x, pz, c), y),
            device_id_type=MESH,
        )

    def z_stay(q):
        first, size = PARTS[q]
        cut = pl.ds(first, size)
        return pltpu.make_async_copy(ordered.at[z, :, :, cut], final.at[z, :, :, cut], z_own.at[q])

    def order_z(q, rows):
        first, size = PARTS[q]
        for group in range(NY):
            block = rows[group * 8:(group + 1) * 8, :, first:first + size].reshape(128, size)
            moved = dot(by_z[...], block, ((1,), (0,))).astype(jnp.bfloat16)
            ordered[:, group, :, first:first + size] = moved.reshape(NZ, 16, size)

    def send_z(q):
        for d in (4, 1, 7, 2, 6, 3, 5):
            z_copy(q, d).start()
        z_stay(q).start()

    def wait_z(q):
        first, size = PARTS[q]
        most = final.at[pl.ds(0, NZ - 1), :, :, pl.ds(first, size)]
        pltpu.make_async_copy(most, most, z_recv.at[q]).wait()
        z_stay(q).wait()

    def order_xy(q):
        first, size = PARTS[q]
        for px in range(NX):
            block = final[:, px, :, first:first + size].reshape(128, size)
            moved = dot(by_z[...], block, ((0,), (0,))).astype(jnp.bfloat16)
            sent[px * 8:(px + 1) * 8, :, first:first + size] = moved.reshape(8, 16, size)

    def rows_of(g):
        lane = lax.broadcasted_iota(jnp.int32, (FL, 128), 1)
        for group in range(NY):
            if g == 0:
                block = mid[group * 8:(group + 1) * 8, :, :PAIR_LANES].reshape(128, PAIR_LANES)
                block = dot(by_z[...], block, ((1,), (0,))).astype(jnp.bfloat16)
            else:
                block = final[:, group, :, g * PAIR_LANES:(g + 1) * PAIR_LANES].reshape(128, PAIR_LANES)
            turned = dot(block, to_k[...], ((0,), (0,)))
            for h in range(2):
                real, imag = (turned[(2 * h + k) * FL:(2 * h + k + 1) * FL] for k in range(2))
                even = jnp.where(lane < 64, real[:, :128], imag[:, 128:])
                odd = jnp.where(lane < 64, imag[:, 128:], real[:, :128])
                to = a_last if g == PAIRS - 1 else a_now
                to[0, group * FL:(group + 1) * FL, h * 128:(h + 1) * 128] = even.astype(jnp.bfloat16)
                to[1, group * FL:(group + 1) * FL, h * 128:(h + 1) * 128] = odd.astype(jnp.bfloat16)

    def gather_waves():
        @pl.loop(0, KTOT // 2 // WAVES)
        def _(k):
            for block in range(WAVES):
                waves[pl.ds(block * 64 + k, 1), :] = jnp.full((1, 128), m_ref[k * WAVES + block]).astype(jnp.float32)

    def make_basis(i, block):
        points = jnp.full((64, 128), p_ref[(w * NY + y) * 2 + i]).astype(jnp.float32)
        wave = waves[block * 64:(block + 1) * 64, :]
        lon = lax.broadcasted_iota(jnp.int32, (64, 128), 1).astype(jnp.float32)
        weight = jnp.where(2.0 * wave < points, jnp.where(wave == 0.0, 1.0, 2.0), 0.0)
        cosine, sine = unit_circle(wave, lon, points)
        cos_step, sin_step = unit_circle(wave, 128.0, points)
        to, at = (basis_last, block - 8) if block >= 8 else (basis, block)
        first = at * 128 + i * 64
        second = at * 128 + (1 - i) * 64

        def step(t, now):
            cosine, sine = now
            cut = pl.ds(pl.multiple_of(t * 128, 128), 128)
            to[i, first:first + 64, cut] = cosine.astype(jnp.bfloat16)
            to[i, second:second + 64, cut] = sine.astype(jnp.bfloat16)
            return cosine * cos_step + sine * sin_step, sine * cos_step - cosine * sin_step

        lax.fori_loop(0, TILES, step, (weight * cosine, -weight * sine))

    def bases(lo, hi):
        for n in range(lo, hi):
            make_basis(n % 2, n // 2)

    def multiply(g):
        k = slice(g * 256, (g + 1) * 256)
        for i in range(2):
            def part(cut):
                total[i, :, cut] = dot(a_now[i], basis[i, k, cut], ((1,), (0,))) + (total[i, :, cut] if g else 0.0)

            @pl.loop(0, 5)
            def _(t):
                part(pl.ds(pl.multiple_of(t * 512, 512), 512))

            part(pl.ds(2560, 128))

    def pass_on(q):
        wait_xy(q)
        order_z(q, mid)
        send_z(q)

    spectral(0)
    order_z(0, sent)
    pl.semaphore_wait(barrier, NPEER - 1 + NZ - 1)
    send_z(0)
    spectral(1)
    send_xy(1)
    send_xy(2)
    spectral(2)
    send_xy(3)
    pass_on(1)
    spectral(3)
    send_xy(4)
    pass_on(2)
    spectral(4)
    send_xy(5)
    wait_z(0)
    order_xy(0)
    send_xy(0)
    gather_waves()
    bases(0, 4)
    pass_on(3)
    bases(4, 10)
    pass_on(4)
    bases(10, 16)
    pass_on(5)
    bases(16, 20)
    loads[2].wait()
    wait_xy(0)
    rows_of(0)
    multiply(0)
    wait_z(1)
    wait_z(2)
    rows_of(1)
    multiply(1)
    for g in range(2, PAIRS):
        wait_z(g + 1)
        rows_of(g)
        if g < PAIRS - 1:
            multiply(g)
    for q in range(len(PARTS)):
        first, size = PARTS[q]
        most = mid.at[pl.ds(0, NPEER - 1), :, pl.ds(first, size)]
        pltpu.make_async_copy(most, most, xy_send.at[q]).wait()
        most = final.at[pl.ds(0, NZ - 1), :, :, pl.ds(first, size)]
        pltpu.make_async_copy(most, most, z_send.at[q]).wait()


def move(spectra, legendre_table, m_order, row_points):
    by_peer, by_z, to_k = permutations()
    hbm = pl.BlockSpec(memory_space=pl.ANY)
    smem = pl.BlockSpec(memory_space=pltpu.SMEM)
    n = len(PARTS)
    bf16, f32 = jnp.bfloat16, jnp.float32
    dma = pltpu.SemaphoreType.DMA
    return pl.pallas_call(
        move_kernel,
        out_shape=(
            pltpu.VMEM((2, 4 * FL, ROWPAD), f32),
            pltpu.VMEM((2, 4 * FL, 256), bf16),
            pltpu.VMEM((2, 256, ROWPAD), bf16),
        ),
        in_specs=[smem, smem, hbm, hbm, hbm, hbm, hbm],
        out_specs=(pl.BlockSpec(memory_space=pltpu.VMEM),) * 3,
        scratch_shapes=[
            pltpu.VMEM((WAVES, 2 * FL, DEG), bf16),
            pltpu.VMEM((WAVES, DEG, NLAT), bf16),
            pltpu.VMEM((NLAT, NLAT), bf16),
            pltpu.VMEM((128, 128), bf16),
            pltpu.VMEM((128, 256), bf16),
            pltpu.VMEM((PAIR_LANES, NLAT), bf16),
            pltpu.VMEM((NPEER, 16, LANES), bf16),
            pltpu.VMEM((NPEER, 16, LANES), bf16),
            pltpu.VMEM((NZ, NY, 16, LANES), bf16),
            pltpu.VMEM((NZ, NY, 16, LANES), bf16),
            pltpu.VMEM((2, 4 * FL, 256), bf16),
            pltpu.VMEM((KTOT // 2, 128), f32),
            pltpu.VMEM((2, KTOT - 256, ROWPAD), bf16),
            dma((3 + 2 * PAIRS,)),
            dma((n,)), dma((n,)), dma((n,)),
            dma((n,)), dma((n,)), dma((n,)),
        ],
        compiler_params=pltpu.CompilerParams(
            collective_id=0, has_side_effects=True, vmem_limit_bytes=51 << 20
        ),
    )(m_order, row_points, spectra, legendre_table, by_peer, by_z, to_k)


CUTS = (512, 512, 512, 512, 512, 128)


def finish_kernel(p_ref, total, a_last, basis_last, grid_hbm, grid, grid_sem):
    row = (lax.axis_index("wave") * NY + lax.axis_index("lev")) * 2
    copies = []
    for i in range(2):
        points = p_ref[row + i]
        for t, size in enumerate(CUTS):
            first = sum(CUTS[:t])
            cut = slice(first, first + size)
            field = dot(a_last[i], basis_last[i, :, cut], ((1,), (0,))) + total[i, :, cut]
            lon = lax.broadcasted_iota(jnp.int32, (4 * FL, size), 1) + first
            field = jnp.where(lon < points, field, 0.0).astype(jnp.bfloat16)
            for y in range(NY):
                for f in range(3):
                    grid[i, f, y * 32:(y + 1) * 32, cut] = field[y * FL + f * 32:y * FL + (f + 1) * 32]
            cut = pl.ds(first, size)
            copy = pltpu.make_async_copy(grid.at[i, :, :, cut], grid_hbm.at[i, :, :, cut], grid_sem.at[i * len(CUTS) + t])
            copy.start()
            copies.append(copy)
    for copy in copies:
        copy.wait()


def finish(total, a_last, basis_last, row_points):
    held = pl.BlockSpec(memory_space=pltpu.VMEM)
    return pl.pallas_call(
        finish_kernel,
        out_shape=jax.ShapeDtypeStruct((2, 3, 128, ROWPAD), jnp.bfloat16),
        in_specs=[pl.BlockSpec(memory_space=pltpu.SMEM), held, held, held],
        out_specs=pl.BlockSpec(memory_space=pl.ANY),
        scratch_shapes=[
            pltpu.VMEM((2, 3, 128, ROWPAD), jnp.bfloat16),
            pltpu.SemaphoreType.DMA((2 * len(CUTS),)),
        ],
        compiler_params=pltpu.CompilerParams(vmem_limit_bytes=12 << 20),
    )(row_points, *(pltpu.with_memory_space_constraint(v, pltpu.VMEM) for v in (total, a_last, basis_last)))


def shards(spectra, legendre_table, m_order, row_points):
    spectra = spectra.reshape(WAVES, 2 * FL, DEG)
    held = move(spectra, legendre_table, m_order, row_points)
    return finish(*held, row_points)


def solution(mesh):
    in_specs = (P("wave", None, None, "lev", None), P("wave", None, None), P(), P())
    out_specs = P(("wave", "lev"), None, None, None)
    return jax.shard_map(shards, mesh=mesh, in_specs=in_specs, out_specs=out_specs, check_vma=False)
```

```python
import functools
import math

import jax
import jax.numpy as jnp
import numpy as np
from jax import lax
from jax.experimental import pallas as pl
from jax.experimental.pallas import tpu as pltpu
from jax.sharding import PartitionSpec as P

MESH = pl.DeviceIdType.MESH
NX, NY, NZ, NC = 4, 4, 8, 2
NPEER = NX * NY * NC
WAVES = 10
PAIRS = WAVES // 2
FL = 96
PAIR_LANES = 4 * FL
LANES = PAIRS * PAIR_LANES
DEG = 640
NLAT = 512
ROWPAD = 2688
TILES = ROWPAD // 128
KTOT = 1280
PARTS = ((0, 384), (384, 128), (512, 256), (768, 384), (1152, 384), (1536, 384))


def permutations():
    by_peer = np.zeros((NLAT, NLAT), np.float32)
    for x in range(NX):
        for y in range(NY):
            for c in range(NC):
                for z in range(NZ):
                    for i in range(2):
                        row = ((x * NZ + z) * NC + c) * 8 + y * 2 + i
                        by_peer[(((x * NY + y) * NC + c) * NZ + z) * 2 + i, row] = 1
    by_z = np.zeros((128, 128), np.float32)
    to_k = np.zeros((128, 256), np.float32)
    for s in range(8):
        for z in range(NZ):
            for i in range(2):
                wave = (s // 2 * NZ + z) * NC + s % 2
                by_z[z * 16 + i * 8 + s, s * 16 + z * 2 + i] = 1
                to_k[z * 16 + i * 8 + s, i * 64 + wave] = 1
                to_k[z * 16 + i * 8 + s, 128 + (1 - i) * 64 + wave] = 1
    return tuple(jnp.asarray(a, jnp.bfloat16) for a in (by_peer, by_z, to_k))


def dot(a, b, dims):
    return lax.dot_general(a, b, (dims, ((), ())), preferred_element_type=jnp.float32)


def unit_circle(wave, lon, points):
    inverse = 1.0 / points
    turns = wave * lon
    residue = turns - jnp.floor(turns * inverse) * points
    residue = jnp.where(residue < 0.0, residue + points, residue)
    residue = jnp.where(residue >= points, residue - points, residue)
    folded = jnp.minimum(residue, points - residue)
    u = (points - 4.0 * folded) * ((0.5 * math.pi) * inverse)
    v = u * u
    cosine, sine = jnp.full_like(u, 1.0 / math.factorial(13)), jnp.full_like(u, 1.0 / math.factorial(14))
    for n in range(6):
        cosine = cosine * -v + 1.0 / math.factorial(11 - 2 * n)
        sine = sine * -v + 1.0 / math.factorial(12 - 2 * n)
    sine = 1.0 - v * sine
    cosine = cosine * u
    sine = jnp.where(2.0 * residue <= points, sine, -sine)
    return cosine, sine


def move_kernel(
    m_ref, p_ref, spec_hbm, leg_hbm, by_peer_hbm, by_z_hbm, to_k_hbm,
    total, a_last, basis_last,
    spec, leg, by_peer, by_z, to_k, coef, sent, mid, ordered, final, a_now,
    waves, basis,
    in_sem, xy_send, xy_recv, xy_own, z_send, z_recv, z_own,
):
    w, y = lax.axis_index("wave"), lax.axis_index("lev")
    x, z, c = w // 16, lax.rem(w // 2, 8), lax.rem(w, 2)

    ys = [lax.rem(y + d, NY) for d in range(NY)]

    def each_peer(act):
        @pl.loop(0, NX)
        def _(d):
            px = lax.rem(x + d, NX)

            @pl.when(d > 0)
            def _():
                act(px, y, c)

            for py in ys[1:]:
                act(px, py, c)
            for py in ys:
                act(px, py, 1 - c)

    def wave_of(px, pz, pc):
        return (px * NZ + pz) * NC + pc

    loads = [
        pltpu.make_async_copy(by_peer_hbm, by_peer, in_sem.at[0]),
        pltpu.make_async_copy(by_z_hbm, by_z, in_sem.at[1]),
        pltpu.make_async_copy(to_k_hbm, to_k, in_sem.at[2]),
    ]
    fetch = []
    for g in range(PAIRS):
        cut = pl.ds(2 * g, 2)
        fetch.append((
            pltpu.make_async_copy(spec_hbm.at[cut], spec.at[cut], in_sem.at[3 + 2 * g]),
            pltpu.make_async_copy(leg_hbm.at[cut], leg.at[cut], in_sem.at[4 + 2 * g]),
        ))
    for f in (*fetch[0], *loads[:2]):
        f.start()

    barrier = pltpu.get_barrier_semaphore()

    @pl.loop(1, NZ)
    def _(d):
        pl.semaphore_signal(barrier, inc=1, device_id=(wave_of(x, lax.rem(z + d, NZ), c), y), device_id_type=MESH)

    def greet(px, py, pc):
        pl.semaphore_signal(barrier, inc=1, device_id=(wave_of(px, z, pc), py), device_id_type=MESH)

    each_peer(greet)
    for f in (*sum(fetch[1:], ()), loads[2]):
        f.start()
    for f in loads[:2]:
        f.wait()
    slot = y * 8 + x * 2 + c
    own = (x * NY + y) * NC + c

    def spectral(g):
        for f in fetch[g]:
            f.wait()
        for h in range(2):
            r = 2 * g + h
            top = DEG - m_ref[w * WAVES + r]
            degree = lax.broadcasted_iota(jnp.int32, (2 * FL, DEG), 1)
            trimmed = jnp.where(degree < top, spec[r], jnp.zeros((), jnp.bfloat16))
            coef[h * 2 * FL:(h + 1) * 2 * FL, :] = dot(trimmed, leg[r], ((1,), (0,))).astype(jnp.bfloat16)
        moved = dot(by_peer[...], coef[...], ((1,), (1,))).astype(jnp.bfloat16)
        sent[:, :, g * PAIR_LANES:(g + 1) * PAIR_LANES] = moved.reshape(NPEER, 16, PAIR_LANES)

    def send_xy(q):
        first, size = PARTS[q]
        cut = pl.ds(first, size)

        def send(px, py, pc):
            pltpu.make_async_remote_copy(
                src_ref=sent.at[(px * NY + py) * NC + pc, :, cut],
                dst_ref=mid.at[slot, :, cut],
                send_sem=xy_send.at[q],
                recv_sem=xy_recv.at[q],
                device_id=(wave_of(px, z, pc), py),
                device_id_type=MESH,
            ).start()

        each_peer(send)
        pltpu.make_async_copy(sent.at[own, :, cut], mid.at[slot, :, cut], xy_own.at[q]).start()

    def wait_xy(q):
        first, size = PARTS[q]
        cut = pl.ds(first, size)
        most = mid.at[pl.ds(0, NPEER - 1), :, cut]
        pltpu.make_async_copy(most, most, xy_recv.at[q]).wait()
        pltpu.make_async_copy(sent.at[own, :, cut], mid.at[slot, :, cut], xy_own.at[q]).wait()

    def z_copy(q, d):
        pz = lax.rem(z + d + (NZ - 2 * d) * c, NZ)
        return pltpu.make_async_remote_copy(
            src_ref=ordered[q].at[pz],
            dst_ref=final[q].at[z],
            send_sem=z_send.at[q],
            recv_sem=z_recv.at[q],
            device_id=(wave_of(x, pz, c), y),
            device_id_type=MESH,
        )

    def z_stay(q):
        return pltpu.make_async_copy(ordered[q].at[z], final[q].at[z], z_own.at[q])

    def order_z(q, rows):
        first, size = PARTS[q]
        for group in range(NY):
            block = rows[group * 8:(group + 1) * 8, :, first:first + size].reshape(128, size)
            moved = dot(by_z[...], block, ((1,), (0,))).astype(jnp.bfloat16)
            ordered[q][:, group] = moved.reshape(NZ, 16, size)

    def send_z(q):
        for d in (4, 1, 7, 2, 6, 3, 5):
            z_copy(q, d).start()
        z_stay(q).start()

    def wait_z(q):
        most = final[q].at[pl.ds(0, NZ - 1)]
        pltpu.make_async_copy(most, most, z_recv.at[q]).wait()
        z_stay(q).wait()

    def order_xy(q):
        first, size = PARTS[q]
        for px in range(NX):
            block = final[q][:, px].reshape(128, size)
            moved = dot(by_z[...], block, ((0,), (0,))).astype(jnp.bfloat16)
            sent[px * 8:(px + 1) * 8, :, first:first + size] = moved.reshape(8, 16, size)

    def rows_of(g):
        lane = lax.broadcasted_iota(jnp.int32, (FL, 128), 1)
        for group in range(NY):
            if g == 0:
                block = mid[group * 8:(group + 1) * 8, :, :PAIR_LANES].reshape(128, PAIR_LANES)
                block = dot(by_z[...], block, ((1,), (0,))).astype(jnp.bfloat16)
            else:
                here = [q for q, (first, _) in enumerate(PARTS) if first // PAIR_LANES == g]
                block = jnp.concatenate([final[q][:, group].reshape(128, PARTS[q][1]) for q in here], axis=1)
            turned = dot(block, to_k[...], ((0,), (0,)))
            for h in range(2):
                real, imag = (turned[(2 * h + k) * FL:(2 * h + k + 1) * FL] for k in range(2))
                even = jnp.where(lane < 64, real[:, :128], imag[:, 128:])
                odd = jnp.where(lane < 64, imag[:, 128:], real[:, :128])
                to = a_last if g == PAIRS - 1 else a_now
                to[0, group * FL:(group + 1) * FL, h * 128:(h + 1) * 128] = even.astype(jnp.bfloat16)
                to[1, group * FL:(group + 1) * FL, h * 128:(h + 1) * 128] = odd.astype(jnp.bfloat16)

    def gather_waves():
        @pl.loop(0, KTOT // 2 // WAVES)
        def _(k):
            for block in range(WAVES):
                waves[pl.ds(block * 64 + k, 1), :] = jnp.full((1, 128), m_ref[k * WAVES + block]).astype(jnp.float32)

    def make_basis(i, block):
        points = jnp.full((64, 128), p_ref[(w * NY + y) * 2 + i]).astype(jnp.float32)
        wave = waves[block * 64:(block + 1) * 64, :]
        lon = lax.broadcasted_iota(jnp.int32, (64, 128), 1).astype(jnp.float32)
        weight = jnp.where(2.0 * wave < points, jnp.where(wave == 0.0, 1.0, 2.0), 0.0)
        cosine, sine = unit_circle(wave, lon, points)
        cos_step, sin_step = unit_circle(wave, 128.0, points)
        to, at = (basis_last, block - 8) if block >= 8 else (basis, block)
        first = at * 128 + i * 64
        second = at * 128 + (1 - i) * 64

        def step(t, now):
            cosine, sine = now
            cut = pl.ds(pl.multiple_of(t * 128, 128), 128)
            to[i, first:first + 64, cut] = cosine.astype(jnp.bfloat16)
            to[i, second:second + 64, cut] = sine.astype(jnp.bfloat16)
            return cosine * cos_step + sine * sin_step, sine * cos_step - cosine * sin_step

        lax.fori_loop(0, TILES, step, (weight * cosine, -weight * sine))

    def bases(lo, hi):
        for n in range(lo, hi):
            make_basis(n % 2, n // 2)

    def multiply(g):
        k = slice(g * 256, (g + 1) * 256)
        for i in range(2):
            def part(cut):
                total[i, :, cut] = dot(a_now[i], basis[i, k, cut], ((1,), (0,))) + (total[i, :, cut] if g else 0.0)

            @pl.loop(0, 5)
            def _(t):
                part(pl.ds(pl.multiple_of(t * 512, 512), 512))

            part(pl.ds(2560, 128))

    def pass_on(q):
        wait_xy(q)
        order_z(q, mid)
        send_z(q)

    spectral(0)
    order_z(0, sent)
    pl.semaphore_wait(barrier, NPEER - 1 + NZ - 1)
    send_z(0)
    spectral(1)
    send_xy(1)
    send_xy(2)
    spectral(2)
    send_xy(3)
    pass_on(1)
    spectral(3)
    send_xy(4)
    pass_on(2)
    spectral(4)
    send_xy(5)
    wait_z(0)
    order_xy(0)
    send_xy(0)
    gather_waves()
    bases(0, 4)
    pass_on(3)
    bases(4, 10)
    pass_on(4)
    bases(10, 16)
    pass_on(5)
    bases(16, 20)
    loads[2].wait()
    wait_xy(0)
    rows_of(0)
    multiply(0)
    wait_z(1)
    wait_z(2)
    rows_of(1)
    multiply(1)
    for g in range(2, PAIRS):
        wait_z(g + 1)
        rows_of(g)
        if g < PAIRS - 1:
            multiply(g)
    for q in range(len(PARTS)):
        first, size = PARTS[q]
        most = mid.at[pl.ds(0, NPEER - 1), :, pl.ds(first, size)]
        pltpu.make_async_copy(most, most, xy_send.at[q]).wait()
        most = final[q].at[pl.ds(0, NZ - 1)]
        pltpu.make_async_copy(most, most, z_send.at[q]).wait()


def move(spectra, legendre_table, m_order, row_points):
    by_peer, by_z, to_k = permutations()
    hbm = pl.BlockSpec(memory_space=pl.ANY)
    smem = pl.BlockSpec(memory_space=pltpu.SMEM)
    n = len(PARTS)
    bf16, f32 = jnp.bfloat16, jnp.float32
    dma = pltpu.SemaphoreType.DMA
    return pl.pallas_call(
        move_kernel,
        out_shape=(
            pltpu.VMEM((2, 4 * FL, ROWPAD), f32),
            pltpu.VMEM((2, 4 * FL, 256), bf16),
            pltpu.VMEM((2, 256, ROWPAD), bf16),
        ),
        in_specs=[smem, smem, hbm, hbm, hbm, hbm, hbm],
        out_specs=(pl.BlockSpec(memory_space=pltpu.VMEM),) * 3,
        scratch_shapes=[
            pltpu.VMEM((WAVES, 2 * FL, DEG), bf16),
            pltpu.VMEM((WAVES, DEG, NLAT), bf16),
            pltpu.VMEM((NLAT, NLAT), bf16),
            pltpu.VMEM((128, 128), bf16),
            pltpu.VMEM((128, 256), bf16),
            pltpu.VMEM((PAIR_LANES, NLAT), bf16),
            pltpu.VMEM((NPEER, 16, LANES), bf16),
            pltpu.VMEM((NPEER, 16, LANES), bf16),
            tuple(pltpu.VMEM((NZ, NY, 16, size), bf16) for _, size in PARTS),
            tuple(pltpu.VMEM((NZ, NY, 16, size), bf16) for _, size in PARTS),
            pltpu.VMEM((2, 4 * FL, 256), bf16),
            pltpu.VMEM((KTOT // 2, 128), f32),
            pltpu.VMEM((2, KTOT - 256, ROWPAD), bf16),
            dma((3 + 2 * PAIRS,)),
            dma((n,)), dma((n,)), dma((n,)),
            dma((n,)), dma((n,)), dma((n,)),
        ],
        compiler_params=pltpu.CompilerParams(
            collective_id=0, has_side_effects=True, vmem_limit_bytes=51 << 20
        ),
    )(m_order, row_points, spectra, legendre_table, by_peer, by_z, to_k)


CUTS = (512, 512, 512, 512, 512, 128)


def finish_kernel(p_ref, total, a_last, basis_last, grid_hbm, grid, grid_sem):
    row = (lax.axis_index("wave") * NY + lax.axis_index("lev")) * 2
    copies = []
    for i in range(2):
        points = p_ref[row + i]
        for t, size in enumerate(CUTS):
            first = sum(CUTS[:t])
            cut = slice(first, first + size)
            field = dot(a_last[i], basis_last[i, :, cut], ((1,), (0,))) + total[i, :, cut]
            lon = lax.broadcasted_iota(jnp.int32, (4 * FL, size), 1) + first
            field = jnp.where(lon < points, field, 0.0).astype(jnp.bfloat16)
            for y in range(NY):
                for f in range(3):
                    grid[i, f, y * 32:(y + 1) * 32, cut] = field[y * FL + f * 32:y * FL + (f + 1) * 32]
            cut = pl.ds(first, size)
            copy = pltpu.make_async_copy(grid.at[i, :, :, cut], grid_hbm.at[i, :, :, cut], grid_sem.at[i * len(CUTS) + t])
            copy.start()
            copies.append(copy)
    for copy in copies:
        copy.wait()


def finish(total, a_last, basis_last, row_points):
    held = pl.BlockSpec(memory_space=pltpu.VMEM)
    return pl.pallas_call(
        finish_kernel,
        out_shape=jax.ShapeDtypeStruct((2, 3, 128, ROWPAD), jnp.bfloat16),
        in_specs=[pl.BlockSpec(memory_space=pltpu.SMEM), held, held, held],
        out_specs=pl.BlockSpec(memory_space=pl.ANY),
        scratch_shapes=[
            pltpu.VMEM((2, 3, 128, ROWPAD), jnp.bfloat16),
            pltpu.SemaphoreType.DMA((2 * len(CUTS),)),
        ],
        compiler_params=pltpu.CompilerParams(vmem_limit_bytes=12 << 20),
    )(row_points, *(pltpu.with_memory_space_constraint(v, pltpu.VMEM) for v in (total, a_last, basis_last)))


def shards(spectra, legendre_table, m_order, row_points):
    spectra = spectra.reshape(WAVES, 2 * FL, DEG)
    held = move(spectra, legendre_table, m_order, row_points)
    return finish(*held, row_points)


def solution(mesh):
    in_specs = (P("wave", None, None, "lev", None), P("wave", None, None), P(), P())
    out_specs = P(("wave", "lev"), None, None, None)
    return jax.shard_map(shards, mesh=mesh, in_specs=in_specs, out_specs=out_specs, check_vma=False)
```
